32 devices in a mesh: kpt: 2 (over y), band: 4 (over x, core), slab: 4 (over z).
Axes of the slice: x: 2, y: 2, z: 4, core: 2. Of those that a mesh axis runs over, the one named last changes fastest.
Arguments:
- wavefunctions: bfloat16 [4, 256, 4, 64, 128], P('band', 'kpt', None, 'slab'), parts along dimension 1, may hold values from -6 to 6
- projectors: bfloat16 [4, 4, 96, 8, 18, 128], P('band', 'slab'), may hold values from -0.09375 to 0.09375
- block_index: int32 [4, 4, 96, 8], P('band', 'slab'), may hold values from -1 to 15, as said below
- proj_counts: int32 [4, 96], P('band'), may hold values from 6 to 18, as said below
- coupling: bfloat16 [4, 96, 18, 18], P('band'), may hold values from -4 to 4
- potential: bfloat16 [4, 64, 128], P('band', 'slab'), may hold values from -1 to 1
Outputs:
- applied: bfloat16 [4, 256, 4, 64, 128], P('band', 'kpt', None, 'slab'), parts along dimension 1
The draws below stay inside these ranges and needn't reach their ends.
There are 2 independent parts, one for each index of `kpt`. The reference program is written for one: setup_inputs(seed, part) draws one part's arguments, and reference() takes and returns one part's arrays. A program takes and returns all parts, laid end to end along the dimension named above; an argument that names none is the same for every part. Nothing has to cross between parts.
Inputs may be any that keep to these rules, and one draw needn't show every extreme that they name: `block_index`: for each region, slab and atom the used slots come first and name distinct blocks; -1 marks an unused slot; every atom uses at least one slot on every slab. `proj_counts`: some atom of every region uses all 18 projectors.
All inputs are finite; a program needn't handle non-finite values.
Results may differ from the reference program's by a relative error of at most 0.0046.
Values may be sent and summed in bfloat16 or wider, within the bound.
A program may use at most 128 MiB of HBM per device.

```python
import jax
import jax.numpy as jnp
from jax import lax

BANDS = 512
NPROJ = 18
AT = 96
BLK = 16
CELLS = 128
SL = 8
REGIONS = 4
GROUPS = 4
SLABS = 4
BPG = 128


def draw_block_index(key, part):
    key = jax.random.fold_in(key, 11)
    total_rows = REGIONS * SLABS * AT
    row_keys = jax.random.split(key, total_rows + 1)
    chosen = jax.vmap(lambda one_key: jax.random.permutation(one_key, BLK)[:SL])(row_keys[:total_rows])
    live = jax.random.randint(row_keys[total_rows], (total_rows, 1), 1, SL + 1)
    slots = jnp.arange(SL, dtype=jnp.int32)[None, :]
    filled = jnp.where(slots < live, chosen.astype(jnp.int32), -1)
    return filled.reshape(REGIONS, SLABS, AT, SL).astype(jnp.int32)


def draw_proj_counts(key, part):
    key = jax.random.fold_in(key, 12)
    first_key, second_key = jax.random.split(key)
    base = jax.random.randint(first_key, (REGIONS, AT), 6, NPROJ + 1)
    marked = jax.random.randint(second_key, (REGIONS,), 0, AT)
    atoms = jnp.arange(AT, dtype=jnp.int32)[None, :]
    return jnp.where(atoms == marked[:, None], NPROJ, base).astype(jnp.int32)


def block_levels(stream_key, shape, pieces, low, largest):
    level, own = 1.0, jax.random.fold_in(stream_key, 6)
    for position, parts in pieces:
        heights = jnp.exp(jax.random.uniform(jax.random.fold_in(own, position), (parts,), jnp.float32, low / len(pieces), largest / len(pieces)))
        level = level * jnp.repeat(heights, shape[position] // parts).reshape([-1 if axis == position else 1 for axis in range(len(shape))])
    return level


def normal_values(own_key, dims, scale, most, cuts=(), kind=jnp.bfloat16):
    array = scale * jax.random.normal(own_key, dims, jnp.float32)
    if cuts:
        array = array * block_levels(own_key, dims, cuts, -0.22, 0.18)
    return jnp.clip(array, -most, most).astype(kind)


def setup_inputs(seed: int = 0, part: int = 0) -> dict:
    key_of = jax.random.split(jax.random.key(seed), 7)
    own_keys = jax.random.split(jax.random.fold_in(key_of[6], part), 7)
    wavefunctions = normal_values(own_keys[0], (GROUPS, BPG, REGIONS, SLABS * BLK, CELLS), 1.0, 6.0, ((0, 4), (3, 4)))
    projectors = normal_values(key_of[1], (REGIONS, SLABS, AT, SL, NPROJ, CELLS), (SL * CELLS * SLABS) ** -0.5, 0.09375, ((0, 4), (1, 4)))
    block_index = draw_block_index(jax.random.fold_in(key_of[6], 71), part)
    proj_counts = draw_proj_counts(jax.random.fold_in(key_of[6], 71), part)
    coupling = normal_values(key_of[4], (REGIONS, AT, NPROJ, NPROJ), 1.0, 4.0, ((0, 4),))
    potential = jnp.clip(jax.random.uniform(key_of[5], (REGIONS, SLABS * BLK, CELLS), jnp.float32, -1.0, 1.0) * block_levels(key_of[5], (REGIONS, SLABS * BLK, CELLS), ((0, 4), (1, 4)), -0.4, 0.0), -1.0, 1.0).astype(jnp.bfloat16)
    return {"wavefunctions": wavefunctions, "projectors": projectors, "block_index": block_index, "proj_counts": proj_counts, "coupling": coupling, "potential": potential}


def region_apply(items):
    psi_region, proj_region, index_region, count_region, coupling_region, potential_region = items
    onehot = (index_region[..., None] == jnp.arange(BLK, dtype=jnp.int32)).astype(jnp.float32)
    keep = (jnp.arange(NPROJ, dtype=jnp.int32)[None, :] < count_region[:, None]).astype(jnp.float32)
    table = jnp.einsum('sajb,sajkp->aksbp', onehot, proj_region.astype(jnp.float32), precision=lax.Precision.HIGHEST)
    table = (table * keep[:, :, None, None, None]).astype(jnp.bfloat16)
    table = lax.optimization_barrier(table).astype(jnp.float32).reshape(AT * NPROJ, SLABS * BLK * CELLS)
    psi = psi_region.reshape(BANDS, SLABS * BLK * CELLS).astype(jnp.float32)
    coefficients = jnp.dot(table, psi.T, precision=lax.Precision.HIGHEST)
    coupled = jnp.einsum('aij,ajn->ain', coupling_region.astype(jnp.float32), coefficients.reshape(AT, NPROJ, BANDS), precision=lax.Precision.HIGHEST)
    coupled = lax.optimization_barrier(coupled.astype(jnp.bfloat16)).astype(jnp.float32).reshape(AT * NPROJ, BANDS)
    local_part = potential_region.reshape(1, SLABS * BLK * CELLS).astype(jnp.float32) * psi
    applied = local_part + jnp.dot(coupled.T, table, precision=lax.Precision.HIGHEST)
    return applied.astype(jnp.bfloat16).reshape(GROUPS, BPG, SLABS * BLK, CELLS)


def reference(wavefunctions, projectors, block_index, proj_counts, coupling, potential):
    by_region = jnp.transpose(wavefunctions, (2, 0, 1, 3, 4))
    result = lax.map(region_apply, (by_region, projectors, block_index, proj_counts, coupling, potential))
    return jnp.transpose(result, (1, 2, 0, 3, 4))
```

```python
import functools

import jax
import jax.numpy as jnp
from jax import lax
from jax.experimental import pallas as pl
from jax.experimental.pallas import tpu as pltpu
from jax.sharding import PartitionSpec as P

MESH = pl.DeviceIdType.MESH


def partner(g, d):
    out, bit = g, 1
    while bit <= d:
        if d & bit:
            out = out + bit - 2 * bit * lax.rem(lax.div(g, bit), 2)
        bit *= 2
    return out


def kernel(dims, psi_ref, proj_ref, idx_ref, cmat_ref, pot_ref, out_ref,
           table, psir, res, part, from_left, from_right, total, mixed, cwide, coupled, flipped,
           psi_send, psi_recv, out_send, out_recv, rs_send, left_recv, right_recv,
           ag_send_r, ag_send_l, ag_recv):
    G, S, NP, AIN, SL, NB, NCH, m = dims
    rows_o = NP * AIN
    rows = S * rows_o
    gpc = G // NCH
    width = gpc * m
    g = lax.axis_index("band")
    s = lax.axis_index("slab")

    barrier = pltpu.get_barrier_semaphore()
    for d in range(1, G):
        pl.semaphore_signal(barrier, inc=1, device_id={"band": partner(g, d)}, device_id_type=MESH)

    @pl.when(s > 0)
    def _():
        pl.semaphore_signal(barrier, inc=1, device_id={"slab": s - 1}, device_id_type=MESH)

    @pl.when(s < S - 1)
    def _():
        pl.semaphore_signal(barrier, inc=1, device_id={"slab": s + 1}, device_id_type=MESH)

    ends = jnp.where(s > 0, 1, 0) + jnp.where(s < S - 1, 1, 0)
    pl.semaphore_wait(barrier, G - 1 + ends)

    def psi_copy(d):
        return pltpu.make_async_remote_copy(
            src_ref=psi_ref.at[partner(g, d)], dst_ref=psir.at[d],
            send_sem=psi_send.at[d], recv_sem=psi_recv.at[d],
            device_id={"band": partner(g, d)}, device_id_type=MESH)

    def out_copy(d):
        return pltpu.make_async_remote_copy(
            src_ref=res.at[d], dst_ref=out_ref.at[g],
            send_sem=out_send.at[d], recv_sem=out_recv.at[d],
            device_id={"band": partner(g, d)}, device_id_type=MESH)

    def rs_copy(c, o, right):
        return pltpu.make_async_remote_copy(
            src_ref=part.at[c, o], dst_ref=(from_left if right else from_right).at[c, o],
            send_sem=rs_send.at[c, o], recv_sem=(left_recv if right else right_recv).at[c, o],
            device_id={"slab": s + 1 if right else s - 1}, device_id_type=MESH)

    def ag_copy(c, o, right):
        return pltpu.make_async_remote_copy(
            src_ref=coupled.at[c, o], dst_ref=coupled.at[c, o],
            send_sem=(ag_send_r if right else ag_send_l).at[c, o], recv_sem=ag_recv.at[c, o],
            device_id={"slab": s + 1 if right else s - 1}, device_id_type=MESH)

    for d in range(1, G):
        psi_copy(d).start()
    psir[0] = psi_ref[g]

    def build(t, carry):
        at = pl.ds(pl.multiple_of(t * 16, 16), 16)
        where_to = idx_ref[at, :]
        slots = [jnp.broadcast_to(where_to[:, j:j + 1], (16, 128)) for j in range(SL)]
        values = [proj_ref[j, at, :].astype(jnp.float32) for j in range(SL)]
        for b in range(NB):
            acc = jnp.zeros((16, 128), jnp.float32)
            for j in range(SL):
                acc = jnp.where(slots[j] == b, values[j], acc)
            table[at, b * 128:(b + 1) * 128] = acc.astype(jnp.bfloat16)
        return carry

    lax.fori_loop(0, rows // 16, build, 0)

    def project(c):
        for d in range(c * gpc, (c + 1) * gpc):
            if d > 0:
                psi_copy(d).wait_recv()

        def one(o, carry):
            at = pl.ds(pl.multiple_of(o * rows_o, rows_o), rows_o)
            psi = psir[c * gpc:(c + 1) * gpc].reshape(width, NB * 128)
            value = lax.dot_general(table[at, :], psi, (((1,), (1,)), ((), ())),
                                    preferred_element_type=jnp.float32)
            part[c, o] = value.astype(jnp.bfloat16)

            @pl.when(o == s)
            def _():
                total[c] = value
            return carry

        lax.fori_loop(0, S, one, 0)

        @pl.when(s == 0)
        def _():
            for o in range(S - 1, 0, -1):
                rs_copy(c, o, True).start()

        @pl.when(s == S - 1)
        def _():
            for o in range(S - 1):
                rs_copy(c, o, False).start()

    def add_in(c, o, box):
        part[c, o] = (part[c, o].astype(jnp.float32) + box[c, o].astype(jnp.float32)).astype(jnp.bfloat16)

    def reduce_on(c):
        for i in range(S - 2):
            o = S - 1 - i

            @pl.when((s > 0) & (s < o))
            def _():
                rs_copy(c, o, True).wait_recv()
                add_in(c, o, from_left)
                rs_copy(c, o, True).start()

            @pl.when((s < S - 1) & (s > i))
            def _():
                rs_copy(c, i, False).wait_recv()
                add_in(c, i, from_right)
                rs_copy(c, i, False).start()

        @pl.when(s > 0)
        def _():
            rs_copy(c, s, True).wait_recv()
            total[c] += from_left[c, s].astype(jnp.float32)

        @pl.when(s < S - 1)
        def _():
            rs_copy(c, s, False).wait_recv()
            total[c] += from_right[c, s].astype(jnp.float32)

        def mix(i, carry):
            acc = jnp.zeros((AIN, width), jnp.float32)
            for j in range(NP):
                acc += cwide[i * NP + j] * total[c, j * AIN:(j + 1) * AIN, :]
            mixed[pl.ds(pl.multiple_of(i * AIN, AIN), AIN), :] = acc
            return carry

        lax.fori_loop(0, NP, mix, 0)
        coupled[c, s] = mixed[...].astype(jnp.bfloat16)

        @pl.when(s < S - 1)
        def _():
            ag_copy(c, s, True).start()

        @pl.when(s > 0)
        def _():
            ag_copy(c, s, False).start()

    def gather_on(c):
        for i in range(1, S):
            @pl.when(s - i >= 0)
            def _():
                ag_copy(c, s - i, True).wait_recv()

                @pl.when(s < S - 1)
                def _():
                    ag_copy(c, s - i, True).start()

            @pl.when(s + i < S)
            def _():
                ag_copy(c, s + i, False).wait_recv()

                @pl.when(s > 0)
                def _():
                    ag_copy(c, s + i, False).start()

    def apply(c):
        flipped[...] = coupled[c].reshape(rows, width).T
        step = 256

        def one(q, carry):
            at = pl.ds(pl.multiple_of(q * step, step), step)
            psi = psir[c * gpc:(c + 1) * gpc, :, at].reshape(width, step)
            value = jnp.dot(flipped[...], table[:, at], preferred_element_type=jnp.float32)
            value += pot_ref[:, at] * psi.astype(jnp.float32)
            value = value.astype(jnp.bfloat16).reshape(gpc, m, step)
            res[c * gpc:(c + 1) * gpc, :, at] = value
            return carry

        lax.fori_loop(0, NB * 128 // step, one, 0)
        for d in range(c * gpc, (c + 1) * gpc):
            if d > 0:
                out_copy(d).start()
            else:
                out_ref[g] = res[0]

    project(0)
    if NCH > 1:
        project(1)
    for ij in range(NP * NP):
        cwide[ij] = jnp.broadcast_to(cmat_ref[:, ij:ij + 1], (AIN, width))
    for c in range(NCH):
        reduce_on(c)
        if c >= 1:
            if c + 1 < NCH:
                project(c + 1)
            gather_on(c - 1)
            apply(c - 1)
    gather_on(NCH - 1)
    apply(NCH - 1)

    for d in range(1, G):
        psi_copy(d).wait_send()
        out_copy(d).wait_send()
        out_copy(d).wait_recv()
    for c in range(NCH):
        for o in range(S):
            @pl.when(s != o)
            def _():
                rs_copy(c, o, True).wait_send()

            @pl.when((s < S - 1) & (s >= o))
            def _():
                ag_copy(c, o, True).wait_send()

            @pl.when((s > 0) & (s <= o))
            def _():
                ag_copy(c, o, False).wait_send()


def on_device(G, S, wavefunctions, projectors, block_index, proj_counts, coupling, potential):
    _, m, regions, NB, cells = wavefunctions.shape
    _, _, AT, SL, NP, _ = projectors.shape
    own = AT // S
    AIN = -(-own // 8) * 8
    NCH = min(4, G)
    rows = S * NP * AIN
    gpc = G // NCH
    width = gpc * m
    s = lax.axis_index("slab")
    psi = jnp.transpose(wavefunctions[0].reshape(m, regions, NB * cells), (1, 0, 2))
    proj = projectors[0, 0].reshape(S, own, SL, NP, cells).transpose(2, 0, 3, 1, 4)
    proj = jnp.pad(proj, ((0, 0), (0, 0), (0, 0), (0, AIN - own), (0, 0))).reshape(SL, rows, cells)
    used = jnp.arange(NP, dtype=jnp.int32)[None, :, None, None] < proj_counts[0].reshape(S, 1, own, 1)
    idx = jnp.where(used, block_index[0, 0].reshape(S, 1, own, SL), -1)
    idx = jnp.pad(idx, ((0, 0), (0, 0), (0, AIN - own), (0, 0)), constant_values=-1).reshape(rows, SL)
    idx = jnp.pad(idx, ((0, 0), (0, 128 - SL)), constant_values=-1)
    cmat = lax.dynamic_slice_in_dim(coupling[0].reshape(AT, NP * NP), s * own, own, 0).astype(jnp.float32)
    cmat = jnp.pad(cmat, ((0, AIN - own), (0, (-NP * NP) % 128)))
    pot = potential.reshape(1, NB * cells).astype(jnp.float32)
    bf = jnp.bfloat16
    rows_o = NP * AIN
    dma = pltpu.SemaphoreType.DMA
    vmem = pl.BlockSpec(memory_space=pltpu.VMEM)
    out = pl.pallas_call(
        functools.partial(kernel, (G, S, NP, AIN, SL, NB, NCH, m)),
        out_shape=jax.ShapeDtypeStruct((G, m, NB * cells), bf),
        in_specs=[vmem] * 5,
        out_specs=vmem,
        scratch_shapes=[
            pltpu.VMEM((rows, NB * cells), bf),
            pltpu.VMEM((G, m, NB * cells), bf),
            pltpu.VMEM((G, m, NB * cells), bf),
            pltpu.VMEM((NCH, S, rows_o, width), bf),
            pltpu.VMEM((NCH, S, rows_o, width), bf),
            pltpu.VMEM((NCH, S, rows_o, width), bf),
            pltpu.VMEM((NCH, rows_o, width), jnp.float32),
            pltpu.VMEM((rows_o, width), jnp.float32),
            pltpu.VMEM((NP * NP, AIN, width), jnp.float32),
            pltpu.VMEM((NCH, S, rows_o, width), bf),
            pltpu.VMEM((width, rows), bf),
            dma((G,)), dma((G,)), dma((G,)), dma((G,)),
            dma((NCH, S)), dma((NCH, S)), dma((NCH, S)),
            dma((NCH, S)), dma((NCH, S)), dma((NCH, S)),
        ],
        compiler_params=pltpu.CompilerParams(
            collective_id=0, has_side_effects=True, vmem_limit_bytes=56 * 1024 * 1024),
        cost_estimate=pl.CostEstimate(
            flops=4 * rows * NB * cells * width * NCH, bytes_accessed=16 << 20, transcendentals=0),
    )(psi, proj, idx, cmat, pot)
    out = jnp.transpose(out, (1, 0, 2)).reshape(1, m, regions, NB, cells)
    return out


def solution(mesh):
    in_specs = (
        P("band", "kpt", None, "slab", None),
        P("band", "slab", None, None, None, None),
        P("band", "slab", None, None),
        P("band", None),
        P("band", None, None, None),
        P("band", "slab", None),
    )
    out_specs = P("band", "kpt", None, "slab", None)
    return jax.shard_map(
        functools.partial(on_device, mesh.shape["band"], mesh.shape["slab"]),
        mesh=mesh, in_specs=in_specs, out_specs=out_specs, check_vma=False)
```

```python
import functools

import jax
import jax.numpy as jnp
from jax import lax
from jax.experimental import pallas as pl
from jax.experimental.pallas import tpu as pltpu
from jax.sharding import PartitionSpec as P

MESH = pl.DeviceIdType.MESH


def partner(g, d):
    out, bit = g, 1
    while bit <= d:
        if d & bit:
            out = out + bit - 2 * bit * lax.rem(lax.div(g, bit), 2)
        bit *= 2
    return out


def kernel(dims, psi_ref, proj_ref, idx_ref, cmat_ref, pot_ref, out_ref,
           table, psir, res, part, from_left, from_right, total, mixed, cwide, coupled, flipped,
           psi_send, psi_recv, out_send, out_recv, rs_send, left_recv, right_recv,
           ag_send_r, ag_send_l, ag_recv):
    G, S, NP, AIN, SL, NB, NCH, m = dims
    rows_o = NP * AIN
    rows = S * rows_o
    gpc = G // NCH
    width = gpc * m
    g = lax.axis_index("band")
    s = lax.axis_index("slab")

    barrier = pltpu.get_barrier_semaphore()
    for d in range(1, G):
        pl.semaphore_signal(barrier, inc=1, device_id={"band": partner(g, d)}, device_id_type=MESH)

    @pl.when(s > 0)
    def _():
        pl.semaphore_signal(barrier, inc=1, device_id={"slab": s - 1}, device_id_type=MESH)

    @pl.when(s < S - 1)
    def _():
        pl.semaphore_signal(barrier, inc=1, device_id={"slab": s + 1}, device_id_type=MESH)

    ends = jnp.where(s > 0, 1, 0) + jnp.where(s < S - 1, 1, 0)
    pl.semaphore_wait(barrier, G - 1 + ends)

    def psi_copy(d):
        return pltpu.make_async_remote_copy(
            src_ref=psi_ref.at[partner(g, d)], dst_ref=psir.at[d],
            send_sem=psi_send.at[d], recv_sem=psi_recv.at[d],
            device_id={"band": partner(g, d)}, device_id_type=MESH)

    def out_copy(d):
        return pltpu.make_async_remote_copy(
            src_ref=res.at[d], dst_ref=out_ref.at[g],
            send_sem=out_send.at[d], recv_sem=out_recv.at[d],
            device_id={"band": partner(g, d)}, device_id_type=MESH)

    def rs_copy(c, o, right):
        return pltpu.make_async_remote_copy(
            src_ref=part.at[c, o], dst_ref=(from_left if right else from_right).at[c, o],
            send_sem=rs_send.at[c, o], recv_sem=(left_recv if right else right_recv).at[c, o],
            device_id={"slab": s + 1 if right else s - 1}, device_id_type=MESH)

    def ag_copy(c, o, right):
        return pltpu.make_async_remote_copy(
            src_ref=coupled.at[c, o], dst_ref=coupled.at[c, o],
            send_sem=(ag_send_r if right else ag_send_l).at[c, o], recv_sem=ag_recv.at[c, o],
            device_id={"slab": s + 1 if right else s - 1}, device_id_type=MESH)

    order = [0, 2, 3, 1] if NCH == 4 else list(range(NCH))
    late = range(3 * gpc, G) if NCH == 4 else range(0)
    for d in range(1, G):
        if d not in late:
            psi_copy(d).start()
    psir[0] = psi_ref[g]

    def build(t, carry):
        at = pl.ds(pl.multiple_of(t * 16, 16), 16)
        where_to = idx_ref[at, :]
        slots = [jnp.broadcast_to(where_to[:, j:j + 1], (16, 128)).astype(jnp.bfloat16) for j in range(SL)]
        values = [proj_ref[j, at, :] for j in range(SL)]
        for b in range(NB):
            acc = jnp.zeros((16, 128), jnp.bfloat16)
            for j in range(SL):
                acc = jnp.where(slots[j] == jnp.bfloat16(b), values[j], acc)
            table[at, b * 128:(b + 1) * 128] = acc
        return carry

    lax.fori_loop(0, rows // 16, build, 0)

    def project(c):
        for d in range(c * gpc, (c + 1) * gpc):
            if d > 0:
                psi_copy(d).wait_recv()

        def one(o, carry):
            at = pl.ds(pl.multiple_of(o * rows_o, rows_o), rows_o)
            psi = psir[c * gpc:(c + 1) * gpc].reshape(width, NB * 128)
            value = lax.dot_general(table[at, :], psi, (((1,), (1,)), ((), ())),
                                    preferred_element_type=jnp.float32)
            part[c, o] = value.astype(jnp.bfloat16)

            @pl.when(o == s)
            def _():
                total[c] = value
            return carry

        lax.fori_loop(0, S, one, 0)

    def start_ends(c):
        @pl.when(s == 0)
        def _():
            rs_copy(c, S - 1, True).start()

        @pl.when(s == S - 1)
        def _():
            rs_copy(c, 0, False).start()

    def add_in(c, o, box):
        part[c, o] = (part[c, o].astype(jnp.float32) + box[c, o].astype(jnp.float32)).astype(jnp.bfloat16)

    def reduce_hop(c, tick):
        @pl.when(s <= tick)
        def _():
            o = S - 1 - tick + s

            @pl.when(s > 0)
            def _():
                rs_copy(c, o, True).wait_recv()
                add_in(c, o, from_left)

            @pl.when(s < tick)
            def _():
                rs_copy(c, o + 1, True).wait_send()
            rs_copy(c, o, True).start()

        @pl.when(S - 1 - s <= tick)
        def _():
            o = tick - (S - 1 - s)

            @pl.when(s < S - 1)
            def _():
                rs_copy(c, o, False).wait_recv()
                add_in(c, o, from_right)

            @pl.when(S - 1 - s < tick)
            def _():
                rs_copy(c, o - 1, False).wait_send()
            rs_copy(c, o, False).start()

    def finish(c):
        @pl.when(s > 0)
        def _():
            rs_copy(c, s, True).wait_recv()
            total[c] += from_left[c, s].astype(jnp.float32)

        @pl.when(s < S - 1)
        def _():
            rs_copy(c, s, False).wait_recv()
            total[c] += from_right[c, s].astype(jnp.float32)

        def mix(i, carry):
            acc = jnp.zeros((AIN, width), jnp.float32)
            for j in range(NP):
                acc += cwide[i * NP + j] * total[c, j * AIN:(j + 1) * AIN, :]
            mixed[pl.ds(pl.multiple_of(i * AIN, AIN), AIN), :] = acc
            return carry

        lax.fori_loop(0, NP, mix, 0)
        coupled[c, s] = mixed[...].astype(jnp.bfloat16)

        @pl.when(s < S - 1)
        def _():
            ag_copy(c, s, True).start()

        @pl.when(s > 0)
        def _():
            ag_copy(c, s, False).start()

    def gather_hop(c, i):
        @pl.when(s - i >= 0)
        def _():
            ag_copy(c, s - i, True).wait_recv()

            @pl.when(s < S - 1)
            def _():
                ag_copy(c, s - i, True).start()

        @pl.when(s + i < S)
        def _():
            ag_copy(c, s + i, False).wait_recv()

            @pl.when(s > 0)
            def _():
                ag_copy(c, s + i, False).start()

    def apply(c):
        flipped[...] = coupled[c].reshape(rows, width).T
        step = 256

        def one(q, carry):
            at = pl.ds(pl.multiple_of(q * step, step), step)
            psi = psir[c * gpc:(c + 1) * gpc, :, at].reshape(width, step)
            value = jnp.dot(flipped[...], table[:, at], preferred_element_type=jnp.float32)
            value += pot_ref[:, at].astype(jnp.float32) * psi.astype(jnp.float32)
            value = value.astype(jnp.bfloat16).reshape(gpc, m, step)
            res[c * gpc:(c + 1) * gpc, :, at] = value
            return carry

        lax.fori_loop(0, NB * 128 // step, one, 0)
        for d in range(c * gpc, (c + 1) * gpc):
            if d > 0:
                out_copy(d).start()
            else:
                out_ref[g] = res[0]

    project(order[0])
    start_ends(order[0])
    for d in late:
        psi_copy(d - gpc).wait_send()
        psi_copy(d).start()
    for n in range(1, min(2, NCH)):
        project(order[n])
    for ij in range(NP * NP):
        cwide[ij] = jnp.broadcast_to(cmat_ref[:, ij:ij + 1], (AIN, width))
    for n in range(NCH):
        for i in range(S - 1):
            if i > 0:
                reduce_hop(order[n], i)
            if n >= 1:
                gather_hop(order[n - 1], i + 1)
        if n + 1 < NCH:
            start_ends(order[n + 1])
        finish(order[n])
        if n >= 1:
            apply(order[n - 1])
        if n + 2 < NCH:
            project(order[n + 2])
    for i in range(1, S):
        gather_hop(order[NCH - 1], i)
    apply(order[NCH - 1])

    for d in range(1, G):
        if d + gpc not in late:
            psi_copy(d).wait_send()
        out_copy(d).wait_send()
        out_copy(d).wait_recv()
    for c in range(NCH):
        for o in range(S):
            @pl.when((s == o - 1) | (s == o + 1))
            def _():
                rs_copy(c, o, True).wait_send()

            @pl.when((s < S - 1) & (s >= o))
            def _():
                ag_copy(c, o, True).wait_send()

            @pl.when((s > 0) & (s <= o))
            def _():
                ag_copy(c, o, False).wait_send()


def on_device(G, S, wavefunctions, projectors, block_index, proj_counts, coupling, potential):
    _, m, regions, NB, cells = wavefunctions.shape
    _, _, AT, SL, NP, _ = projectors.shape
    own = AT // S
    AIN = -(-own // 8) * 8
    NCH = min(4, G)
    rows = S * NP * AIN
    gpc = G // NCH
    width = gpc * m
    s = lax.axis_index("slab")
    psi = jnp.transpose(wavefunctions[0].reshape(m, regions, NB * cells), (1, 0, 2))
    proj = projectors[0, 0].reshape(S, own, SL, NP, cells).transpose(2, 0, 3, 1, 4)
    proj = jnp.pad(proj, ((0, 0), (0, 0), (0, 0), (0, AIN - own), (0, 0))).reshape(SL, rows, cells)
    used = jnp.arange(NP, dtype=jnp.int32)[None, :, None, None] < proj_counts[0].reshape(S, 1, own, 1)
    idx = jnp.where(used, block_index[0, 0].reshape(S, 1, own, SL), -1)
    idx = jnp.pad(idx, ((0, 0), (0, 0), (0, AIN - own), (0, 0)), constant_values=-1).reshape(rows, SL)
    idx = jnp.pad(idx, ((0, 0), (0, 128 - SL)), constant_values=-1).astype(jnp.float32)
    cmat = lax.dynamic_slice_in_dim(coupling[0].reshape(AT, NP * NP), s * own, own, 0).astype(jnp.float32)
    cmat = jnp.pad(cmat, ((0, AIN - own), (0, (-NP * NP) % 128)))
    pot = potential.reshape(1, NB * cells)
    bf = jnp.bfloat16
    rows_o = NP * AIN
    dma = pltpu.SemaphoreType.DMA
    vmem = pl.BlockSpec(memory_space=pltpu.VMEM)
    out = pl.pallas_call(
        functools.partial(kernel, (G, S, NP, AIN, SL, NB, NCH, m)),
        out_shape=jax.ShapeDtypeStruct((G, m, NB * cells), bf),
        in_specs=[vmem] * 5,
        out_specs=vmem,
        scratch_shapes=[
            pltpu.VMEM((rows, NB * cells), bf),
            pltpu.VMEM((G, m, NB * cells), bf),
            pltpu.VMEM((G, m, NB * cells), bf),
            pltpu.VMEM((NCH, S, rows_o, width), bf),
            pltpu.VMEM((NCH, S, rows_o, width), bf),
            pltpu.VMEM((NCH, S, rows_o, width), bf),
            pltpu.VMEM((NCH, rows_o, width), jnp.float32),
            pltpu.VMEM((rows_o, width), jnp.float32),
            pltpu.VMEM((NP * NP, AIN, width), jnp.float32),
            pltpu.VMEM((NCH, S, rows_o, width), bf),
            pltpu.VMEM((width, rows), bf),
            dma((G,)), dma((G,)), dma((G,)), dma((G,)),
            dma((NCH, S)), dma((NCH, S)), dma((NCH, S)),
            dma((NCH, S)), dma((NCH, S)), dma((NCH, S)),
        ],
        compiler_params=pltpu.CompilerParams(
            collective_id=0, has_side_effects=True, vmem_limit_bytes=56 * 1024 * 1024),
        cost_estimate=pl.CostEstimate(
            flops=4 * rows * NB * cells * width * NCH, bytes_accessed=16 << 20, transcendentals=0),
    )(psi, proj, idx, cmat, pot)
    out = jnp.transpose(out, (1, 0, 2)).reshape(1, m, regions, NB, cells)
    return out


def solution(mesh):
    in_specs = (
        P("band", "kpt", None, "slab", None),
        P("band", "slab", None, None, None, None),
        P("band", "slab", None, None),
        P("band", None),
        P("band", None, None, None),
        P("band", "slab", None),
    )
    out_specs = P("band", "kpt", None, "slab", None)
    return jax.shard_map(
        functools.partial(on_device, mesh.shape["band"], mesh.shape["slab"]),
        mesh=mesh, in_specs=in_specs, out_specs=out_specs, check_vma=False)
```

```python
import functools

import jax
import jax.numpy as jnp
from jax import lax
from jax.experimental import pallas as pl
from jax.experimental.pallas import tpu as pltpu
from jax.sharding import PartitionSpec as P

MESH = pl.DeviceIdType.MESH


def partner(g, d):
    out, bit = g, 1
    while bit <= d:
        if d & bit:
            out = out + bit - 2 * bit * lax.rem(lax.div(g, bit), 2)
        bit *= 2
    return out


def kernel(dims, psi_ref, proj_ref, idx_ref, cmat_ref, pot_ref, out_ref,
           table, psir, res, part, from_left, from_right, total, mixed, cwide, coupled, flipped,
           psi_send, psi_recv, out_send, out_recv, rs_send, left_recv, right_recv,
           ag_send_r, ag_send_l, ag_recv):
    G, S, NP, AIN, SL, NB, NCH, m = dims
    rows_o = NP * AIN
    rows = S * rows_o
    gpc = G // NCH
    width = gpc * m
    g = lax.axis_index("band")
    s = lax.axis_index("slab")

    barrier = pltpu.get_barrier_semaphore()
    for d in range(1, G):
        pl.semaphore_signal(barrier, inc=1, device_id={"band": partner(g, d)}, device_id_type=MESH)

    @pl.when(s > 0)
    def _():
        pl.semaphore_signal(barrier, inc=1, device_id={"slab": s - 1}, device_id_type=MESH)

    @pl.when(s < S - 1)
    def _():
        pl.semaphore_signal(barrier, inc=1, device_id={"slab": s + 1}, device_id_type=MESH)

    ends = jnp.where(s > 0, 1, 0) + jnp.where(s < S - 1, 1, 0)
    pl.semaphore_wait(barrier, G - 1 + ends)

    def psi_copy(d):
        return pltpu.make_async_remote_copy(
            src_ref=psi_ref.at[partner(g, d)], dst_ref=psir.at[d],
            send_sem=psi_send.at[d], recv_sem=psi_recv.at[d],
            device_id={"band": partner(g, d)}, device_id_type=MESH)

    def out_copy(d):
        return pltpu.make_async_remote_copy(
            src_ref=res.at[d], dst_ref=out_ref.at[g],
            send_sem=out_send.at[d], recv_sem=out_recv.at[d],
            device_id={"band": partner(g, d)}, device_id_type=MESH)

    def rs_copy(c, o, right):
        return pltpu.make_async_remote_copy(
            src_ref=part.at[c, o], dst_ref=(from_left if right else from_right).at[c, o],
            send_sem=rs_send.at[c, o], recv_sem=(left_recv if right else right_recv).at[c, o],
            device_id={"slab": s + 1 if right else s - 1}, device_id_type=MESH)

    def ag_copy(c, o, right):
        return pltpu.make_async_remote_copy(
            src_ref=coupled.at[c, o], dst_ref=coupled.at[c, o],
            send_sem=(ag_send_r if right else ag_send_l).at[c, o], recv_sem=ag_recv.at[c, o],
            device_id={"slab": s + 1 if right else s - 1}, device_id_type=MESH)

    order = [0, 2, 3, 1] if NCH == 4 else list(range(NCH))
    late = range(3 * gpc, G) if NCH == 4 else range(0)
    for d in range(1, G):
        if d not in late:
            psi_copy(d).start()
    psir[0] = psi_ref[g]

    def build(t, carry):
        at = pl.ds(pl.multiple_of(t * 16, 16), 16)
        where_to = idx_ref[at, :]
        slots = [jnp.broadcast_to(where_to[:, j:j + 1], (16, 128)).astype(jnp.bfloat16) for j in range(SL)]
        values = [proj_ref[j, at, :] for j in range(SL)]
        for b in range(NB):
            acc = jnp.zeros((16, 128), jnp.bfloat16)
            for j in range(SL):
                acc = jnp.where(slots[j] == jnp.bfloat16(b), values[j], acc)
            table[at, b * 128:(b + 1) * 128] = acc
        return carry

    lax.fori_loop(0, rows // 16, build, 0, unroll=4)

    def project(c):
        for d in range(c * gpc, (c + 1) * gpc):
            if d > 0:
                psi_copy(d).wait_recv()

        def one(o, carry):
            at = pl.ds(pl.multiple_of(o * rows_o, rows_o), rows_o)
            psi = psir[c * gpc:(c + 1) * gpc].reshape(width, NB * 128)
            value = lax.dot_general(table[at, :], psi, (((1,), (1,)), ((), ())),
                                    preferred_element_type=jnp.float32)
            part[c, o] = value.astype(jnp.bfloat16)

            @pl.when(o == s)
            def _():
                total[c] = value
            return carry

        lax.fori_loop(0, S, one, 0)

    def start_ends(c):
        @pl.when(s == 0)
        def _():
            rs_copy(c, S - 1, True).start()

        @pl.when(s == S - 1)
        def _():
            rs_copy(c, 0, False).start()

    def add_in(c, o, box):
        part[c, o] = (part[c, o].astype(jnp.float32) + box[c, o].astype(jnp.float32)).astype(jnp.bfloat16)

    def reduce_hop(c, tick):
        @pl.when(s <= tick)
        def _():
            o = S - 1 - tick + s

            @pl.when(s > 0)
            def _():
                rs_copy(c, o, True).wait_recv()
                add_in(c, o, from_left)

            @pl.when(s < tick)
            def _():
                rs_copy(c, o + 1, True).wait_send()
            rs_copy(c, o, True).start()

        @pl.when(S - 1 - s <= tick)
        def _():
            o = tick - (S - 1 - s)

            @pl.when(s < S - 1)
            def _():
                rs_copy(c, o, False).wait_recv()
                add_in(c, o, from_right)

            @pl.when(S - 1 - s < tick)
            def _():
                rs_copy(c, o - 1, False).wait_send()
            rs_copy(c, o, False).start()

    def finish(c):
        @pl.when(s > 0)
        def _():
            rs_copy(c, s, True).wait_recv()
            total[c] += from_left[c, s].astype(jnp.float32)

        @pl.when(s < S - 1)
        def _():
            rs_copy(c, s, False).wait_recv()
            total[c] += from_right[c, s].astype(jnp.float32)

        def mix(i, carry):
            acc = jnp.zeros((AIN, width), jnp.float32)
            for j in range(NP):
                acc += cwide[i * NP + j] * total[c, j * AIN:(j + 1) * AIN, :]
            mixed[pl.ds(pl.multiple_of(i * AIN, AIN), AIN), :] = acc
            return carry

        lax.fori_loop(0, NP, mix, 0)
        coupled[c, s] = mixed[...].astype(jnp.bfloat16)

        @pl.when(s < S - 1)
        def _():
            ag_copy(c, s, True).start()

        @pl.when(s > 0)
        def _():
            ag_copy(c, s, False).start()

    def gather_hop(c, i):
        @pl.when(s - i >= 0)
        def _():
            ag_copy(c, s - i, True).wait_recv()

            @pl.when(s < S - 1)
            def _():
                ag_copy(c, s - i, True).start()

        @pl.when(s + i < S)
        def _():
            ag_copy(c, s + i, False).wait_recv()

            @pl.when(s > 0)
            def _():
                ag_copy(c, s + i, False).start()

    def apply(c):
        flipped[...] = coupled[c].reshape(rows, width).T
        step = 256

        def one(q, carry):
            at = pl.ds(pl.multiple_of(q * step, step), step)
            psi = psir[c * gpc:(c + 1) * gpc, :, at].reshape(width, step)
            value = jnp.dot(flipped[...], table[:, at], preferred_element_type=jnp.float32)
            value += pot_ref[:, at].astype(jnp.float32) * psi.astype(jnp.float32)
            value = value.astype(jnp.bfloat16).reshape(gpc, m, step)
            res[c * gpc:(c + 1) * gpc, :, at] = value
            return carry

        lax.fori_loop(0, NB * 128 // step, one, 0)
        for d in range(c * gpc, (c + 1) * gpc):
            if d > 0:
                out_copy(d).start()
            else:
                out_ref[g] = res[0]

    project(order[0])
    start_ends(order[0])
    for d in late:
        psi_copy(d - gpc).wait_send()
        psi_copy(d).start()
    for n in range(1, min(2, NCH)):
        project(order[n])
    for ij in range(NP * NP):
        cwide[ij] = jnp.broadcast_to(cmat_ref[:, ij:ij + 1], (AIN, width))
    for n in range(NCH):
        for i in range(S - 1):
            if i > 0:
                reduce_hop(order[n], i)
            if n >= 1:
                gather_hop(order[n - 1], i + 1)
        if n + 1 < NCH:
            start_ends(order[n + 1])
        finish(order[n])
        if n >= 1:
            apply(order[n - 1])
        if n + 2 < NCH:
            project(order[n + 2])
    for i in range(1, S):
        gather_hop(order[NCH - 1], i)
    apply(order[NCH - 1])

    for d in range(1, G):
        if d + gpc not in late:
            psi_copy(d).wait_send()
        out_copy(d).wait_send()
        out_copy(d).wait_recv()
    for c in range(NCH):
        for o in range(S):
            @pl.when((s == o - 1) | (s == o + 1))
            def _():
                rs_copy(c, o, True).wait_send()

            @pl.when((s < S - 1) & (s >= o))
            def _():
                ag_copy(c, o, True).wait_send()

            @pl.when((s > 0) & (s <= o))
            def _():
                ag_copy(c, o, False).wait_send()


def on_device(G, S, wavefunctions, projectors, block_index, proj_counts, coupling, potential):
    _, m, regions, NB, cells = wavefunctions.shape
    _, _, AT, SL, NP, _ = projectors.shape
    own = AT // S
    AIN = -(-own // 8) * 8
    NCH = min(4, G)
    rows = S * NP * AIN
    gpc = G // NCH
    width = gpc * m
    s = lax.axis_index("slab")
    psi = jnp.transpose(wavefunctions[0].reshape(m, regions, NB * cells), (1, 0, 2))
    proj = projectors[0, 0].reshape(S, own, SL, NP, cells).transpose(2, 0, 3, 1, 4)
    proj = jnp.pad(proj, ((0, 0), (0, 0), (0, 0), (0, AIN - own), (0, 0))).reshape(SL, rows, cells)
    used = jnp.arange(NP, dtype=jnp.int32)[None, :, None, None] < proj_counts[0].reshape(S, 1, own, 1)
    idx = jnp.where(used, block_index[0, 0].reshape(S, 1, own, SL), -1)
    idx = jnp.pad(idx, ((0, 0), (0, 0), (0, AIN - own), (0, 0)), constant_values=-1).reshape(rows, SL)
    idx = jnp.pad(idx, ((0, 0), (0, 128 - SL)), constant_values=-1).astype(jnp.float32)
    cmat = lax.dynamic_slice_in_dim(coupling[0].reshape(AT, NP * NP), s * own, own, 0).astype(jnp.float32)
    cmat = jnp.pad(cmat, ((0, AIN - own), (0, (-NP * NP) % 128)))
    pot = potential.reshape(1, NB * cells)
    bf = jnp.bfloat16
    rows_o = NP * AIN
    dma = pltpu.SemaphoreType.DMA
    vmem = pl.BlockSpec(memory_space=pltpu.VMEM)
    out = pl.pallas_call(
        functools.partial(kernel, (G, S, NP, AIN, SL, NB, NCH, m)),
        out_shape=jax.ShapeDtypeStruct((G, m, NB * cells), bf),
        in_specs=[vmem] * 5,
        out_specs=vmem,
        scratch_shapes=[
            pltpu.VMEM((rows, NB * cells), bf),
            pltpu.VMEM((G, m, NB * cells), bf),
            pltpu.VMEM((G, m, NB * cells), bf),
            pltpu.VMEM((NCH, S, rows_o, width), bf),
            pltpu.VMEM((NCH, S, rows_o, width), bf),
            pltpu.VMEM((NCH, S, rows_o, width), bf),
            pltpu.VMEM((NCH, rows_o, width), jnp.float32),
            pltpu.VMEM((rows_o, width), jnp.float32),
            pltpu.VMEM((NP * NP, AIN, width), jnp.float32),
            pltpu.VMEM((NCH, S, rows_o, width), bf),
            pltpu.VMEM((width, rows), bf),
            dma((G,)), dma((G,)), dma((G,)), dma((G,)),
            dma((NCH, S)), dma((NCH, S)), dma((NCH, S)),
            dma((NCH, S)), dma((NCH, S)), dma((NCH, S)),
        ],
        compiler_params=pltpu.CompilerParams(
            collective_id=0, has_side_effects=True, vmem_limit_bytes=56 * 1024 * 1024),
        cost_estimate=pl.CostEstimate(
            flops=4 * rows * NB * cells * width * NCH, bytes_accessed=16 << 20, transcendentals=0),
    )(psi, proj, idx, cmat, pot)
    out = jnp.transpose(out, (1, 0, 2)).reshape(1, m, regions, NB, cells)
    return out


def solution(mesh):
    in_specs = (
        P("band", "kpt", None, "slab", None),
        P("band", "slab", None, None, None, None),
        P("band", "slab", None, None),
        P("band", None),
        P("band", None, None, None),
        P("band", "slab", None),
    )
    out_specs = P("band", "kpt", None, "slab", None)
    return jax.shard_map(
        functools.partial(on_device, mesh.shape["band"], mesh.shape["slab"]),
        mesh=mesh, in_specs=in_specs, out_specs=out_specs, check_vma=False)
```
